256 devices in a mesh: samp: 2 (over x_lo), lat: 16 (over z, core), lon: 8 (over x_hi, y).
Axes of the slice: x: 4 (x_hi: 2, x_lo: 2; x = x_hi * 2 + x_lo), y: 4, z: 8, core: 2. Of those that a mesh axis runs over, the one named last changes fastest.
Arguments:
- tokens: bfloat16 [512, 512, 512], P(('samp', 'lat'), 'lon'), parts along dimension 0, may hold values from -6 to 6
- block_gain: float32 [512], replicated, may hold values from 0.25 to 1.75
- block_qkv: bfloat16 [512, 1536], replicated, may hold values from -16 to 16
- block_out: bfloat16 [512, 512], replicated, may hold values from -0.25 to 0.25
- grid_gain: float32 [512], replicated, may hold values from 0.25 to 1.75
- grid_qkv: bfloat16 [512, 1536], replicated, may hold values from -16 to 16
- grid_out: bfloat16 [512, 512], replicated, may hold values from -0.25 to 0.25
- mlp_gain: float32 [512], replicated, may hold values from 0.25 to 1.75
- w_up: bfloat16 [512, 2048], replicated, may hold values from -0.25 to 0.25
- w_down: bfloat16 [2048, 512], replicated, may hold values from -0.125 to 0.125
Outputs:
- blocks_out: bfloat16 [512, 512, 512], P(('samp', 'lat'), 'lon'), parts along dimension 0
The draws below stay inside these ranges and needn't reach their ends.
There are 2 independent parts, one for each index of `samp`. The reference program is written for one: setup_inputs(seed, part) draws one part's arguments, and reference() takes and returns one part's arrays. A program takes and returns all parts, laid end to end along the dimension named above; an argument that names none is the same for every part. Nothing has to cross between parts.
All inputs are finite; a program needn't handle non-finite values.
Results may differ from the reference program's by a relative error of at most 0.015.
Values may be sent and summed in bfloat16 or wider, within the bound.
A program may use at most 64 MiB of HBM per device.

```python
import math
import jax
import jax.numpy as jnp
from jax import lax

D = 512
HEADS = 16
FF = 2048
WIN = 8
H = 256
W = 512


def qkv_base(key):
    return jax.random.truncated_normal(key, -3.0, 3.0, (D, 3 * D), jnp.float32) / math.sqrt(D)


def draw_block_qkv(key, part):
    key = jax.random.fold_in(key, 11)
    base = qkv_base(key)
    return base.astype(jnp.bfloat16)


def draw_grid_qkv(key, part):
    key = jax.random.fold_in(key, 23)
    base = qkv_base(key)
    return base.astype(jnp.bfloat16)


def block_levels(stream_key, dims, pieces, least, top_value):
    def one(position, shards_of):
        heights = jax.random.uniform(jax.random.fold_in(jax.random.fold_in(stream_key, 6), position), (shards_of,), jnp.float32, least / len(pieces), top_value / len(pieces))
        return jnp.repeat(jnp.exp(heights), dims[position] // shards_of).reshape((-1,) + (1,) * (len(dims) - position - 1))

    level = one(*pieces[0])
    for cut in pieces[1:]:
        level = level * one(*cut)
    return level


def noise(stream_key, dims, scale, reach, cuts=(), held_as=jnp.bfloat16):
    entries = jax.random.normal(stream_key, dims, jnp.float32) * scale
    if len(cuts) > 0:
        entries = block_levels(stream_key, dims, cuts, -0.22, 0.18) * entries
    return jnp.clip(entries, min=-reach, max=reach).astype(held_as)


def setup_inputs(seed: int = 0, part: int = 0) -> dict:
    arg_keys = jax.random.split(jax.random.key(seed), 11)
    part_splits = jax.random.split(jax.random.fold_in(arg_keys[10], part), 11)
    tokens = noise(part_splits[0], (H, W, D), 1.0, 6.0, ((0, 16), (1, 8)))
    block_gain = jnp.clip(1.0 + 0.15 * jax.random.normal(arg_keys[1], (D,), jnp.float32), 0.25, 1.75)
    block_qkv = draw_block_qkv(jax.random.fold_in(arg_keys[10], 71), part)
    block_out = noise(arg_keys[3], (D, D), D ** -0.5, 0.25)
    grid_gain = jnp.clip(1.0 + 0.15 * jax.random.normal(arg_keys[4], (D,), jnp.float32), 0.25, 1.75)
    grid_qkv = draw_grid_qkv(jax.random.fold_in(arg_keys[10], 71), part)
    grid_out = noise(arg_keys[6], (D, D), D ** -0.5, 0.25)
    mlp_gain = jnp.clip(1.0 + 0.15 * jax.random.normal(arg_keys[7], (D,), jnp.float32), 0.25, 1.75)
    w_up = noise(arg_keys[8], (D, FF), D ** -0.5, 0.25)
    w_down = noise(arg_keys[9], (FF, D), FF ** -0.5, 0.125)
    return {"tokens": tokens, "block_gain": block_gain, "block_qkv": block_qkv, "block_out": block_out, "grid_gain": grid_gain, "grid_qkv": grid_qkv, "grid_out": grid_out, "mlp_gain": mlp_gain, "w_up": w_up, "w_down": w_down}


def layer_norm(tile, gain):
    values = tile.astype(jnp.float32)
    row_mean = lax.optimization_barrier(jnp.mean(values, axis=-1, keepdims=True))
    centred = values - row_mean
    spread = lax.optimization_barrier(jnp.mean(centred * centred, axis=-1, keepdims=True))
    return (centred * lax.rsqrt(spread + 1e-05) * gain).astype(jnp.bfloat16)

def window_attention(windows, gain, w_qkv, w_proj):
    count, span, width = windows.shape
    head_size = width // HEADS
    normed = layer_norm(windows, gain)
    projected = jnp.dot(normed.reshape(count * span, width), w_qkv, preferred_element_type=jnp.float32)
    projected = projected.astype(jnp.bfloat16).reshape(count, span, 3, HEADS, head_size)
    queries = projected[:, :, 0].astype(jnp.float32)
    keys_all = projected[:, :, 1].astype(jnp.float32)
    values_all = projected[:, :, 2].astype(jnp.float32)
    scores = jnp.einsum('nqhe,nkhe->nhqk', queries, keys_all) * (1.0 / math.sqrt(head_size))
    weights_soft = jax.nn.softmax(scores, axis=-1).astype(jnp.bfloat16)
    mixed = jnp.einsum('nhqk,nkhe->nqhe', weights_soft.astype(jnp.float32), values_all)
    mixed = mixed.astype(jnp.bfloat16).reshape(count * span, width)
    result = jnp.dot(mixed, w_proj, preferred_element_type=jnp.float32).reshape(count, span, width)
    return (windows.astype(jnp.float32) + result).astype(jnp.bfloat16)

def to_blocks(tile):
    rows, cols, width = tile.shape
    shaped = tile.reshape(rows // WIN, WIN, cols // WIN, WIN, width)
    return shaped.transpose(0, 2, 1, 3, 4).reshape(-1, WIN * WIN, width)

def from_blocks(windows, rows, cols):
    width = windows.shape[-1]
    shaped = windows.reshape(rows // WIN, cols // WIN, WIN, WIN, width)
    return shaped.transpose(0, 2, 1, 3, 4).reshape(rows, cols, width)

def to_grid(tile):
    rows, cols, width = tile.shape
    shaped = tile.reshape(WIN, rows // WIN, WIN, cols // WIN, width)
    return shaped.transpose(1, 3, 0, 2, 4).reshape(-1, WIN * WIN, width)

def from_grid(windows, rows, cols):
    width = windows.shape[-1]
    shaped = windows.reshape(rows // WIN, cols // WIN, WIN, WIN, width)
    return shaped.transpose(2, 0, 3, 1, 4).reshape(rows, cols, width)

def feed_forward(tile, gain, w_up, w_down):
    rows, cols, width = tile.shape
    normed = layer_norm(tile, gain).reshape(rows * cols, width)
    hidden = jax.nn.gelu(jnp.dot(normed, w_up, preferred_element_type=jnp.float32), approximate=True).astype(jnp.bfloat16)
    result = jnp.dot(hidden, w_down, preferred_element_type=jnp.float32).reshape(rows, cols, width)
    return (tile.astype(jnp.float32) + result).astype(jnp.bfloat16)

def reference(tokens, block_gain, block_qkv, block_out, grid_gain, grid_qkv, grid_out, mlp_gain, w_up, w_down):
    rows, cols, width = tokens.shape
    after_block = from_blocks(window_attention(to_blocks(tokens), block_gain, block_qkv, block_out), rows, cols)
    after_grid = from_grid(window_attention(to_grid(after_block), grid_gain, grid_qkv, grid_out), rows, cols)
    return feed_forward(after_grid, mlp_gain, w_up, w_down)
```

```python
import math

import jax
import jax.numpy as jnp
from jax import lax
from jax.experimental import pallas as pl
from jax.experimental.pallas import tpu as pltpu
from jax.sharding import PartitionSpec as P

MESH = pl.DeviceIdType.MESH
BF16 = jnp.bfloat16
F32 = jnp.float32

HEADS = 16
WIN = 8
D = 512
FF = 2048
HEAD = D // HEADS
SPAN = WIN * WIN
HALVES = 2
GROUP = 4
ROWS = GROUP * SPAN
ZN = 8
LONS = 8
LANES = 128
QUAD = LANES // HEAD
SCALE = math.log2(math.e) / math.sqrt(HEAD)


def norm(x, gain):
    mean = jnp.mean(x, axis=-1, keepdims=True)
    centred = x - mean
    spread = jnp.mean(centred * centred, axis=-1, keepdims=True)
    return (centred * lax.rsqrt(spread + 1e-05) * gain).astype(BF16)


def head_masks():
    lane = lax.broadcasted_iota(jnp.int32, (SPAN, LANES), 1)
    return [(lane >= h * HEAD) & (lane < (h + 1) * HEAD) for h in range(QUAD)]


def attend(load, gain, w_qkv, w_out, q_s, k_s, v_s, mixed_s):
    normed = norm(load(), gain[...])
    q_s[...] = (jnp.dot(normed, w_qkv[:, :D], preferred_element_type=F32) * SCALE).astype(BF16)
    k_s[...] = jnp.dot(normed, w_qkv[:, D : 2 * D], preferred_element_type=F32).astype(BF16)
    v_s[...] = jnp.dot(normed, w_qkv[:, 2 * D :], preferred_element_type=F32).astype(BF16)
    masks = head_masks()
    for w in range(GROUP):
        rows = slice(w * SPAN, (w + 1) * SPAN)
        for g in range(HEADS // QUAD):
            cols = slice(g * LANES, (g + 1) * LANES)
            q = q_s[rows, cols]
            diagonal = jnp.concatenate([jnp.where(m, q, jnp.zeros_like(q)) for m in masks], axis=0)
            scores = lax.dot_general(
                k_s[rows, cols], diagonal, (((1,), (1,)), ((), ())), preferred_element_type=F32
            )
            probs = jnp.exp2(scores - jnp.max(scores, axis=0, keepdims=True))
            probs = (probs * (1.0 / jnp.sum(probs, axis=0, keepdims=True))).astype(BF16)
            mixed = lax.dot_general(
                probs, v_s[rows, cols], (((0,), (0,)), ((), ())), preferred_element_type=F32
            )
            kept = mixed[(QUAD - 1) * SPAN :]
            for h in range(QUAD - 1):
                kept = jnp.where(masks[h], mixed[h * SPAN : (h + 1) * SPAN], kept)
            mixed_s[rows, cols] = kept.astype(BF16)
    return load() + jnp.dot(mixed_s[...], w_out[...], preferred_element_type=F32)


def kernel(
    tokens, block_gain, block_qkv, block_out, grid_gain, grid_qkv, grid_out, mlp_gain, w_up, w_down,
    out,
    x_s, g1, wq1, wo1, g2, wq2, wo2, g3, wu, wd,
    q_s, k_s, v_s, mixed_s, xf, yf,
    send_a, recv_a, send_b, recv_b, out_s,
    load_sem, out_sem, sa, ra, sb, rb,
):
    lat = lax.axis_index("lat")
    lon = lax.axis_index("lon")
    z = lat // 2
    core = lax.rem(lat, 2)
    y = lax.rem(lon, 4)
    xh = lon // 4

    def peer(pz, plon):
        return {"lat": pz * 2 + core, "lon": plon}

    def loads(half):
        return pltpu.make_async_copy(
            tokens.at[pl.ds(half * WIN, WIN)], x_s.at[pl.ds(half * WIN, WIN)], load_sem.at[half]
        )

    weights = [
        pltpu.make_async_copy(src, dst, load_sem.at[HALVES + i])
        for i, (src, dst) in enumerate([
            (block_gain, g1), (block_qkv, wq1), (block_out, wo1),
            (grid_gain, g2), (grid_qkv, wq2), (grid_out, wo2),
            (mlp_gain, g3), (w_up, wu), (w_down, wd),
        ])
    ]
    loads(0).start()
    for copy in weights[:3]:
        copy.start()
    loads(1).start()
    for copy in weights[3:]:
        copy.start()

    def step_of(i):
        return ((i + 1) // 2) * (2 * lax.rem(i, 2) - 1)

    barrier = pltpu.get_barrier_semaphore()

    def greet(i, carry):
        pz = lax.rem(z + step_of(lax.rem(i, ZN)) + ZN, ZN)
        plon = lax.rem(lon + i // ZN, LONS)

        @pl.when(i != 0)
        def _():
            pl.semaphore_signal(barrier, inc=1, device_id=peer(pz, plon), device_id_type=MESH)

        return carry

    lax.fori_loop(0, ZN * LONS, greet, 0)

    mine = z * LONS + lon

    def send(src, dst, send_sem, recv_sem, pz, plon):
        local = (pz == z) & (plon == lon)

        @pl.when(local)
        def _():
            pltpu.make_async_copy(src, dst, recv_sem).start()

        @pl.when(jnp.logical_not(local))
        def _():
            pltpu.make_async_remote_copy(
                src_ref=src, dst_ref=dst, send_sem=send_sem, recv_sem=recv_sem,
                device_id=peer(pz, plon), device_id_type=MESH,
            ).start()

    first = lax.rem(z + xh + y, 2)

    def block_phase(s, carry):
        half = s // 2
        side = lax.rem(s + first, 2)

        @pl.when(s == 0)
        def _():
            loads(0).wait()
            for copy in weights[:3]:
                copy.wait()

        @pl.when(s == 2)
        def _():
            loads(1).wait()

        def load():
            tile = x_s[pl.ds(half * WIN, WIN), pl.ds(pl.multiple_of(side * 32, 32), 32), :].astype(F32)
            return jnp.concatenate(
                [tile[:, w * WIN : (w + 1) * WIN, :].reshape(SPAN, D) for w in range(GROUP)], axis=0
            )

        result = attend(load, g1, wq1, wo1, q_s, k_s, v_s, mixed_s)
        for w in range(GROUP):
            part = result[w * SPAN : (w + 1) * SPAN].reshape(WIN, WIN, D)
            for r in range(WIN):
                send_a[(half * ZN + r) * LONS + side * GROUP + w] = part[r].astype(BF16)

        @pl.when(s == 0)
        def _():
            pl.semaphore_wait(barrier, ZN * LONS - 1)

        def sends(i, carry):
            pz = lax.rem(z + step_of(lax.rem(i, ZN)) + ZN, ZN)
            plon = side * GROUP + lax.rem(y + i // ZN, GROUP)
            send(
                send_a.at[pl.ds((half * ZN + pz) * LONS + plon, 1)],
                recv_a.at[pl.ds(half * ZN * LONS + mine, 1)],
                sa, ra.at[half], pz, plon,
            )
            return carry

        lax.fori_loop(0, ZN * GROUP, sends, 0)
        return carry

    lax.fori_loop(0, 2 * HALVES, block_phase, 0)

    for copy in weights[3:6]:
        copy.wait()

    def grid_phase(half, carry):
        arrived = recv_a.at[pl.ds(half * ZN * LONS, ZN * LONS)]
        pltpu.make_async_copy(arrived, arrived, ra.at[half]).wait()
        for c in range(D // LANES):
            cols = slice(c * LANES, (c + 1) * LANES)
            xf[c] = arrived[:, :, cols].astype(F32).reshape(ZN * LONS * WIN, LANES)

        def four(j, carry):
            def load():
                return jnp.concatenate(
                    [
                        jnp.concatenate(
                            [xf[c, pl.ds(j * GROUP + w, SPAN, stride=WIN), :] for c in range(D // LANES)],
                            axis=1,
                        )
                        for w in range(GROUP)
                    ],
                    axis=0,
                )

            result = attend(load, g2, wq2, wo2, q_s, k_s, v_s, mixed_s)
            for w in range(GROUP):
                for c in range(D // LANES):
                    yf[c, pl.ds(j * GROUP + w, SPAN, stride=WIN), :] = result[
                        w * SPAN : (w + 1) * SPAN, c * LANES : (c + 1) * LANES
                    ]
            return carry

        lax.fori_loop(0, 2, four, 0)
        for c in range(D // LANES):
            send_b[pl.ds(half * ZN * LONS, ZN * LONS), :, c * LANES : (c + 1) * LANES] = (
                yf[c].reshape(ZN * LONS, WIN, LANES).astype(BF16)
            )

        def sends(i, carry):
            pz = lax.rem(z + step_of(lax.rem(i, ZN)) + ZN, ZN)
            plon = lax.rem(lon + i // ZN, LONS)
            send(
                send_b.at[pl.ds((half * ZN + pz) * LONS + plon, 1)],
                recv_b.at[pl.ds(half * ZN * LONS + mine, 1)],
                sb, rb.at[half], pz, plon,
            )
            return carry

        lax.fori_loop(0, ZN * LONS, sends, 0)
        return carry

    lax.fori_loop(0, HALVES, grid_phase, 0)

    for copy in weights[6:]:
        copy.wait()

    per = ROWS // (LONS * WIN)

    def outs(t):
        return pltpu.make_async_copy(
            out_s.at[pl.ds(t * per, per)], out.at[pl.ds(t * per, per)], out_sem.at[t]
        )

    def mlp_phase(t, carry):
        half = t // 2

        @pl.when(lax.rem(t, 2) == 0)
        def _():
            arrived = recv_b.at[pl.ds(half * ZN * LONS, ZN * LONS)]
            pltpu.make_async_copy(arrived, arrived, rb.at[half]).wait()

        def load():
            return recv_b[pl.ds(t * per * LONS, per * LONS)].astype(F32).reshape(ROWS, D)

        normed = norm(load(), g3[...])
        total = load()
        for f in range(FF // D):
            cols = slice(f * D, (f + 1) * D)
            hidden = jax.nn.gelu(
                jnp.dot(normed, wu[:, cols], preferred_element_type=F32), approximate=True
            ).astype(BF16)
            total = total + jnp.dot(hidden, wd[cols, :], preferred_element_type=F32)
        out_s[pl.ds(t * per, per)] = total.astype(BF16).reshape(per, LONS * WIN, D)
        outs(t).start()
        return carry

    lax.fori_loop(0, 2 * HALVES, mlp_phase, 0)

    for t in range(2 * HALVES):
        outs(t).wait()
    gone = send_a.at[pl.ds(0, ZN * LONS * HALVES - HALVES)]
    pltpu.make_async_copy(gone, gone, sa).wait()
    gone = send_b.at[pl.ds(0, ZN * LONS * HALVES - HALVES)]
    pltpu.make_async_copy(gone, gone, sb).wait()


def shards(
    tokens, block_gain, block_qkv, block_out, grid_gain, grid_qkv, grid_out, mlp_gain, w_up, w_down
):
    rows, cols, width = tokens.shape
    slabs = HALVES * ZN * LONS
    any_spec = pl.BlockSpec(memory_space=pl.ANY)
    vmem = pltpu.VMEM
    return pl.pallas_call(
        kernel,
        out_shape=jax.ShapeDtypeStruct(tokens.shape, BF16),
        in_specs=[any_spec] * 10,
        out_specs=any_spec,
        scratch_shapes=[
            vmem((rows, cols, D), BF16),
            vmem((1, D), F32), vmem((D, 3 * D), BF16), vmem((D, D), BF16),
            vmem((1, D), F32), vmem((D, 3 * D), BF16), vmem((D, D), BF16),
            vmem((1, D), F32), vmem((D, FF), BF16), vmem((FF, D), BF16),
            vmem((ROWS, D), BF16), vmem((ROWS, D), BF16), vmem((ROWS, D), BF16), vmem((ROWS, D), BF16),
            vmem((D // LANES, ZN * LONS * WIN, LANES), F32), vmem((D // LANES, ZN * LONS * WIN, LANES), F32),
            vmem((slabs, WIN, D), BF16), vmem((slabs, WIN, D), BF16),
            vmem((slabs, WIN, D), BF16), vmem((slabs, WIN, D), BF16),
            vmem((rows, cols, D), BF16),
            pltpu.SemaphoreType.DMA((HALVES + 9,)),
            pltpu.SemaphoreType.DMA((2 * HALVES,)),
            pltpu.SemaphoreType.DMA,
            pltpu.SemaphoreType.DMA((HALVES,)),
            pltpu.SemaphoreType.DMA,
            pltpu.SemaphoreType.DMA((HALVES,)),
        ],
        compiler_params=pltpu.CompilerParams(
            collective_id=0, has_side_effects=True, vmem_limit_bytes=48 << 20
        ),
    )(
        tokens, block_gain.reshape(1, D), block_qkv, block_out, grid_gain.reshape(1, D), grid_qkv, grid_out,
        mlp_gain.reshape(1, D), w_up, w_down,
    )


def solution(mesh):
    in_specs = (P(("samp", "lat"), "lon", None), P(), P(), P(), P(), P(), P(), P(), P(), P())
    out_specs = P(("samp", "lat"), "lon", None)
    return jax.shard_map(shards, mesh=mesh, in_specs=in_specs, out_specs=out_specs, check_vma=False)
```

```python
import math

import jax
import jax.numpy as jnp
from jax import lax
from jax.experimental import pallas as pl
from jax.experimental.pallas import tpu as pltpu
from jax.sharding import PartitionSpec as P

MESH = pl.DeviceIdType.MESH
BF16 = jnp.bfloat16
F32 = jnp.float32

HEADS = 16
WIN = 8
D = 512
FF = 2048
HEAD = D // HEADS
SPAN = WIN * WIN
HALVES = 2
GROUP = 4
ROWS = GROUP * SPAN
QUARTERS = 4
ZN = 8
ZHALF = 4
LONS = 8
SLABS = ZN * LONS
PAIR = 2
STEPS = LONS // PAIR
Z_OFFSETS = (1, -1, 2, -2, 3, -3, 4, 0)
LANES = 128
QUAD = LANES // HEAD
SCALE = math.log2(math.e) / math.sqrt(HEAD)


def norm(x, gain):
    mean = jnp.mean(x, axis=-1, keepdims=True)
    centred = x - mean
    spread = jnp.mean(centred * centred, axis=-1, keepdims=True)
    return (centred * lax.rsqrt(spread + 1e-05) * gain).astype(BF16)


def head_masks():
    lane = lax.broadcasted_iota(jnp.int32, (SPAN, LANES), 1)
    return [(lane >= h * HEAD) & (lane < (h + 1) * HEAD) for h in range(QUAD)]


def attend(load, gain, w_qkv, w_out, q_s, k_s, v_s, mixed_s):
    normed = norm(load(), gain[...])
    q_s[...] = (jnp.dot(normed, w_qkv[:, :D], preferred_element_type=F32) * SCALE).astype(BF16)
    k_s[...] = jnp.dot(normed, w_qkv[:, D : 2 * D], preferred_element_type=F32).astype(BF16)
    v_s[...] = jnp.dot(normed, w_qkv[:, 2 * D :], preferred_element_type=F32).astype(BF16)
    masks = head_masks()
    for w in range(GROUP):
        rows = slice(w * SPAN, (w + 1) * SPAN)
        for g in range(HEADS // QUAD):
            cols = slice(g * LANES, (g + 1) * LANES)
            q = q_s[rows, cols]
            diagonal = jnp.concatenate([jnp.where(m, q, jnp.zeros_like(q)) for m in masks], axis=0)
            scores = lax.dot_general(
                k_s[rows, cols], diagonal, (((1,), (1,)), ((), ())), preferred_element_type=F32
            )
            probs = jnp.exp2(scores - jnp.max(scores, axis=0, keepdims=True))
            probs = (probs * (1.0 / jnp.sum(probs, axis=0, keepdims=True))).astype(BF16)
            mixed = lax.dot_general(
                probs, v_s[rows, cols], (((0,), (0,)), ((), ())), preferred_element_type=F32
            )
            kept = mixed[(QUAD - 1) * SPAN :]
            for h in range(QUAD - 1):
                kept = jnp.where(masks[h], mixed[h * SPAN : (h + 1) * SPAN], kept)
            mixed_s[rows, cols] = kept.astype(BF16)
    return load() + jnp.dot(mixed_s[...], w_out[...], preferred_element_type=F32)


def kernel(
    tokens, block_gain, block_qkv, block_out, grid_gain, grid_qkv, grid_out, mlp_gain, w_up, w_down,
    out,
    x_s, g1, wq1, wo1, g2, wq2, wo2, g3, wu, wd,
    q_s, k_s, v_s, mixed_s, xf, yf,
    send_a, recv_a, send_b, recv_b, out_s,
    load_sem, out_sem, sa, ra, sb, rb,
):
    lat = lax.axis_index("lat")
    lon = lax.axis_index("lon")
    z = lat // 2
    core = lax.rem(lat, 2)

    def peer(pz, plon):
        return {"lat": pz * 2 + core, "lon": plon}

    def quarter_load(q):
        part = (pl.ds(q // 2 * WIN, WIN), pl.ds(q % 2 * GROUP * WIN, GROUP * WIN))
        return pltpu.make_async_copy(tokens.at[part], x_s.at[part], load_sem.at[q])

    def around(off):
        return lax.rem(z + off + ZN, ZN)

    barrier = pltpu.get_barrier_semaphore()

    for b in range(LONS):
        plon = lax.rem(lon + b, LONS)
        for off in Z_OFFSETS:
            if b or off:
                pl.semaphore_signal(
                    barrier, inc=1, device_id=peer(around(off), plon), device_id_type=MESH
                )

    weights = [
        pltpu.make_async_copy(src, dst, load_sem.at[QUARTERS + i])
        for i, (src, dst) in enumerate([
            (block_gain, g1), (block_qkv, wq1), (block_out, wo1),
            (grid_gain, g2), (grid_qkv, wq2), (grid_out, wo2),
            (mlp_gain, g3), (w_up, wu), (w_down, wd),
        ])
    ]
    quarter_load(0).start()
    for copy in weights[:3]:
        copy.start()
    for q in range(1, QUARTERS):
        quarter_load(q).start()
    for copy in weights[3:]:
        copy.start()

    mine = z * LONS + lon

    def push(src, dst, send_sem, recv_sem, pz, plon):
        pltpu.make_async_remote_copy(
            src_ref=src, dst_ref=dst, send_sem=send_sem, recv_sem=recv_sem,
            device_id=peer(pz, plon), device_id_type=MESH,
        ).start()

    def push_or_keep(local, src, dst, send_sem, recv_sem, pz, plon):
        @pl.when(local)
        def _():
            pltpu.make_async_copy(src, dst, recv_sem).start()

        @pl.when(jnp.logical_not(local))
        def _():
            push(src, dst, send_sem, recv_sem, pz, plon)

    def arrived(ref, sem):
        pltpu.make_async_copy(ref, ref, sem).wait()

    parity = lax.rem(z, 2)

    def block_phase(q, carry):
        half = q // 2
        side = lax.rem(q, 2)

        @pl.when(q == 0)
        def _():
            for copy in weights[:3]:
                copy.wait()

        for i in range(QUARTERS):
            @pl.when(q == i)
            def _():
                quarter_load(i).wait()

        def load():
            tile = x_s[pl.ds(half * WIN, WIN), pl.ds(pl.multiple_of(side * 32, 32), 32), :].astype(F32)
            return jnp.concatenate(
                [tile[:, w * WIN : (w + 1) * WIN, :].reshape(SPAN, D) for w in range(GROUP)], axis=0
            )

        result = attend(load, g1, wq1, wo1, q_s, k_s, v_s, mixed_s)
        for w in range(GROUP):
            part = result[w * SPAN : (w + 1) * SPAN].reshape(WIN, WIN, D)
            for r in range(WIN):
                send_a[(q * LONS + r) * ZHALF + w] = part[r].astype(BF16)

        @pl.when(q == 0)
        def _():
            pl.semaphore_wait(barrier, SLABS - 1)

        def sends(b, carry):
            plon = lax.rem(lon + b, LONS)
            for i in (1, 3, 2, 0):
                w = lax.rem(z // 2 + i, ZHALF)
                src = send_a.at[pl.ds((q * LONS + plon) * ZHALF + w, 1)]
                dst = recv_a.at[pl.ds(half * SLABS + mine, 1)]
                if i:
                    push(src, dst, sa, ra.at[half], 2 * w + side, plon)
                else:
                    push_or_keep((b == 0) & (side == parity), src, dst, sa, ra.at[half], 2 * w + side, plon)
            return carry

        lax.fori_loop(0, LONS, sends, 0)
        return carry

    lax.fori_loop(0, QUARTERS, block_phase, 0)

    for copy in weights[3:6]:
        copy.wait()

    def grid_phase(half, carry):
        slabs = pl.ds(half * SLABS, SLABS)
        arrived(recv_a.at[slabs], ra.at[half])
        for c in range(D // LANES):
            cols = slice(c * LANES, (c + 1) * LANES)
            xf[c] = recv_a[slabs, :, cols].astype(F32).reshape(SLABS * WIN, LANES)

        def four(j, carry):
            def load():
                return jnp.concatenate(
                    [
                        jnp.concatenate(
                            [xf[c, pl.ds(j * GROUP + w, SPAN, stride=WIN), :] for c in range(D // LANES)],
                            axis=1,
                        )
                        for w in range(GROUP)
                    ],
                    axis=0,
                )

            result = attend(load, g2, wq2, wo2, q_s, k_s, v_s, mixed_s)
            for w in range(GROUP):
                for c in range(D // LANES):
                    yf[c, pl.ds(j * GROUP + w, SPAN, stride=WIN), :] = result[
                        w * SPAN : (w + 1) * SPAN, c * LANES : (c + 1) * LANES
                    ]
            return carry

        lax.fori_loop(0, 2, four, 0)
        for c in range(D // LANES):
            send_b[slabs, :, c * LANES : (c + 1) * LANES] = (
                yf[c].reshape(SLABS, WIN, LANES).astype(BF16)
            )

        def sends(b, carry):
            plon = lax.rem(lon + b, LONS)
            dst = recv_b.at[pl.ds((half * LONS + b) * ZN + parity * ZHALF + z // 2, 1)]
            sem = rb.at[half * STEPS + b // PAIR]
            for off in Z_OFFSETS:
                pz = around(off)
                src = send_b.at[pl.ds(half * SLABS + pz * LONS + plon, 1)]
                if off:
                    push(src, dst, sb, sem, pz, plon)
                else:
                    push_or_keep(b == 0, src, dst, sb, sem, pz, plon)
            return carry

        lax.fori_loop(0, LONS, sends, 0)
        return carry

    lax.fori_loop(0, HALVES, grid_phase, 0)

    for copy in weights[6:]:
        copy.wait()

    def outs(t, i):
        row = t // STEPS * WIN + lax.rem(lon - lax.rem(t, STEPS) * PAIR - i + LONS, LONS)
        return pltpu.make_async_copy(out_s.at[t * PAIR + i], out.at[row], out_sem.at[t])

    def mlp_phase(t, carry):
        slabs = pl.ds(t * (PAIR * ZN), PAIR * ZN)
        arrived(recv_b.at[slabs], rb.at[t])

        def load():
            return recv_b[slabs].astype(F32).reshape(PAIR * SPAN, D)

        normed = norm(load(), g3[...])
        total = load()
        for f in range(FF // D):
            cols = slice(f * D, (f + 1) * D)
            hidden = jax.nn.gelu(
                jnp.dot(normed, wu[:, cols], preferred_element_type=F32), approximate=True
            ).astype(BF16)
            total = total + jnp.dot(hidden, wd[cols, :], preferred_element_type=F32)
        out_s[pl.ds(t * PAIR, PAIR)] = total.astype(BF16).reshape(PAIR, SPAN, D)
        for i in range(PAIR):
            outs(t, i).start()
        return carry

    lax.fori_loop(0, HALVES * STEPS, mlp_phase, 0)

    for t in range(HALVES * STEPS):
        arrived(out_s.at[pl.ds(t * PAIR, PAIR)], out_sem.at[t])
    gone = send_a.at[pl.ds(0, HALVES * (SLABS - 1))]
    arrived(gone, sa)
    arrived(gone, sb)


def shards(
    tokens, block_gain, block_qkv, block_out, grid_gain, grid_qkv, grid_out, mlp_gain, w_up, w_down
):
    rows, cols, width = tokens.shape
    slabs = HALVES * SLABS
    any_spec = pl.BlockSpec(memory_space=pl.ANY)
    vmem = pltpu.VMEM
    return pl.pallas_call(
        kernel,
        out_shape=jax.ShapeDtypeStruct(tokens.shape, BF16),
        in_specs=[any_spec] * 10,
        out_specs=any_spec,
        scratch_shapes=[
            vmem((rows, cols, D), BF16),
            vmem((1, D), F32), vmem((D, 3 * D), BF16), vmem((D, D), BF16),
            vmem((1, D), F32), vmem((D, 3 * D), BF16), vmem((D, D), BF16),
            vmem((1, D), F32), vmem((D, FF), BF16), vmem((FF, D), BF16),
            vmem((ROWS, D), BF16), vmem((ROWS, D), BF16), vmem((ROWS, D), BF16), vmem((ROWS, D), BF16),
            vmem((D // LANES, SLABS * WIN, LANES), F32), vmem((D // LANES, SLABS * WIN, LANES), F32),
            vmem((slabs, WIN, D), BF16), vmem((slabs, WIN, D), BF16),
            vmem((slabs, WIN, D), BF16), vmem((slabs, WIN, D), BF16),
            vmem((rows, cols, D), BF16),
            pltpu.SemaphoreType.DMA((QUARTERS + 9,)),
            pltpu.SemaphoreType.DMA((HALVES * STEPS,)),
            pltpu.SemaphoreType.DMA,
            pltpu.SemaphoreType.DMA((HALVES,)),
            pltpu.SemaphoreType.DMA,
            pltpu.SemaphoreType.DMA((HALVES * STEPS,)),
        ],
        compiler_params=pltpu.CompilerParams(
            collective_id=0, has_side_effects=True, vmem_limit_bytes=48 << 20
        ),
    )(*[pltpu.with_memory_space_constraint(a, pltpu.HBM) for a in (
        tokens, block_gain.reshape(1, D), block_qkv, block_out, grid_gain.reshape(1, D), grid_qkv, grid_out,
        mlp_gain.reshape(1, D), w_up, w_down,
    )])


def solution(mesh):
    in_specs = (P(("samp", "lat"), "lon", None), P(), P(), P(), P(), P(), P(), P(), P(), P())
    out_specs = P(("samp", "lat"), "lon", None)
    return jax.shard_map(shards, mesh=mesh, in_specs=in_specs, out_specs=out_specs, check_vma=False)
```

```python
import math

import jax
import jax.numpy as jnp
from jax import lax
from jax.experimental import pallas as pl
from jax.experimental.pallas import tpu as pltpu
from jax.sharding import PartitionSpec as P

MESH = pl.DeviceIdType.MESH
BF16 = jnp.bfloat16
F32 = jnp.float32

HEADS = 16
WIN = 8
D = 512
FF = 2048
HEAD = D // HEADS
SPAN = WIN * WIN
HALVES = 2
GROUP = 4
ROWS = GROUP * SPAN
QUARTERS = 4
ZN = 8
ZHALF = 4
LONS = 8
SLABS = ZN * LONS
Z_OFFSETS = (1, -1, 2, -2, 3, -3, 4, 0)
LANES = 128
QUAD = LANES // HEAD
SCALE = math.log2(math.e) / math.sqrt(HEAD)


def norm(x, gain):
    mean = jnp.mean(x, axis=-1, keepdims=True)
    centred = x - mean
    spread = jnp.mean(centred * centred, axis=-1, keepdims=True)
    return (centred * lax.rsqrt(spread + 1e-05) * gain).astype(BF16)


def head_masks():
    lane = lax.broadcasted_iota(jnp.int32, (SPAN, LANES), 1)
    return [(lane >= h * HEAD) & (lane < (h + 1) * HEAD) for h in range(QUAD)]


def attend(load, gain, w_qkv, w_out, q_s, k_s, v_s, mixed_s):
    normed = norm(load(), gain[...])
    q_s[...] = (jnp.dot(normed, w_qkv[:, :D], preferred_element_type=F32) * SCALE).astype(BF16)
    k_s[...] = jnp.dot(normed, w_qkv[:, D : 2 * D], preferred_element_type=F32).astype(BF16)
    v_s[...] = jnp.dot(normed, w_qkv[:, 2 * D :], preferred_element_type=F32).astype(BF16)
    masks = head_masks()
    for w in range(GROUP):
        rows = slice(w * SPAN, (w + 1) * SPAN)
        for g in range(HEADS // QUAD):
            cols = slice(g * LANES, (g + 1) * LANES)
            q = q_s[rows, cols]
            diagonal = jnp.concatenate([jnp.where(m, q, jnp.zeros_like(q)) for m in masks], axis=0)
            scores = lax.dot_general(
                k_s[rows, cols], diagonal, (((1,), (1,)), ((), ())), preferred_element_type=F32
            )
            probs = jnp.exp2(scores - jnp.max(scores, axis=0, keepdims=True))
            probs = (probs * (1.0 / jnp.sum(probs, axis=0, keepdims=True))).astype(BF16)
            mixed = lax.dot_general(
                probs, v_s[rows, cols], (((0,), (0,)), ((), ())), preferred_element_type=F32
            )
            kept = mixed[(QUAD - 1) * SPAN :]
            for h in range(QUAD - 1):
                kept = jnp.where(masks[h], mixed[h * SPAN : (h + 1) * SPAN], kept)
            mixed_s[rows, cols] = kept.astype(BF16)
    return load() + jnp.dot(mixed_s[...], w_out[...], preferred_element_type=F32)


def kernel(
    tokens, block_gain, block_qkv, block_out, grid_gain, grid_qkv, grid_out, mlp_gain, w_up, w_down,
    out,
    x_s, g1, wq1, wo1, g2, wq2, wo2, g3, wu, wd,
    q_s, k_s, v_s, mixed_s, xf, yf,
    send_a, recv_a, send_b,
    load_sem, sa, ra, sb, rb,
):
    lat = lax.axis_index("lat")
    lon = lax.axis_index("lon")
    z = lat // 2
    core = lax.rem(lat, 2)

    def peer(pz, plon):
        return {"lat": pz * 2 + core, "lon": plon}

    def quarter_load(q):
        part = (pl.ds(q // 2 * WIN, WIN), pl.ds(q % 2 * GROUP * WIN, GROUP * WIN))
        return pltpu.make_async_copy(tokens.at[part], x_s.at[part], load_sem.at[q])

    def around(off):
        return lax.rem(z + off + ZN, ZN)

    barrier = pltpu.get_barrier_semaphore()

    for b in range(LONS):
        plon = lax.rem(lon + b, LONS)
        for off in Z_OFFSETS:
            if b or off:
                pl.semaphore_signal(
                    barrier, inc=1, device_id=peer(around(off), plon), device_id_type=MESH
                )

    weights = [
        pltpu.make_async_copy(src, dst, load_sem.at[QUARTERS + i])
        for i, (src, dst) in enumerate([
            (block_gain, g1), (block_qkv, wq1), (block_out, wo1),
            (grid_gain, g2), (grid_qkv, wq2), (grid_out, wo2),
            (mlp_gain, g3), (w_up, wu), (w_down, wd),
        ])
    ]
    quarter_load(0).start()
    for copy in weights[:3]:
        copy.start()
    for q in range(1, QUARTERS):
        quarter_load(q).start()
    for copy in weights[3:]:
        copy.start()

    def push(src, dst, send_sem, recv_sem, pz, plon):
        pltpu.make_async_remote_copy(
            src_ref=src, dst_ref=dst, send_sem=send_sem, recv_sem=recv_sem,
            device_id=peer(pz, plon), device_id_type=MESH,
        ).start()

    def push_or_keep(local, src, dst, send_sem, recv_sem, pz, plon):
        @pl.when(local)
        def _():
            pltpu.make_async_copy(src, dst, recv_sem).start()

        @pl.when(jnp.logical_not(local))
        def _():
            push(src, dst, send_sem, recv_sem, pz, plon)

    def arrived(ref, sem):
        pltpu.make_async_copy(ref, ref, sem).wait()

    parity = lax.rem(z, 2)

    def block_phase(q, carry):
        half = q // 2
        side = lax.rem(q, 2)

        @pl.when(q == 0)
        def _():
            for copy in weights[:3]:
                copy.wait()

        for i in range(QUARTERS):
            @pl.when(q == i)
            def _():
                quarter_load(i).wait()

        def load():
            tile = x_s[pl.ds(half * WIN, WIN), pl.ds(pl.multiple_of(side * 32, 32), 32), :].astype(F32)
            return jnp.concatenate(
                [tile[:, w * WIN : (w + 1) * WIN, :].reshape(SPAN, D) for w in range(GROUP)], axis=0
            )

        result = attend(load, g1, wq1, wo1, q_s, k_s, v_s, mixed_s)
        for w in range(GROUP):
            part = result[w * SPAN : (w + 1) * SPAN].reshape(WIN, WIN, D)
            for r in range(WIN):
                send_a[(q * LONS + r) * ZHALF + w] = part[r].astype(BF16)

        @pl.when(q == 0)
        def _():
            pl.semaphore_wait(barrier, SLABS - 1)

        def sends(b, carry):
            plon = lax.rem(lon + b, LONS)
            for i in (1, 3, 2, 0):
                w = lax.rem(z // 2 + i, ZHALF)
                src = send_a.at[pl.ds((q * LONS + plon) * ZHALF + w, 1)]
                dst = recv_a.at[pl.ds(half * SLABS + b * ZN + z, 1)]
                if i:
                    push(src, dst, sa, ra.at[half], 2 * w + side, plon)
                else:
                    push_or_keep((b == 0) & (side == parity), src, dst, sa, ra.at[half], 2 * w + side, plon)
            return carry

        lax.fori_loop(0, LONS, sends, 0)
        return carry

    lax.fori_loop(0, QUARTERS, block_phase, 0)

    for copy in weights[3:]:
        copy.wait()

    def grid_phase(half, carry):
        slabs = pl.ds(half * SLABS, SLABS)
        arrived(recv_a.at[slabs], ra.at[half])
        for c in range(D // LANES):
            cols = slice(c * LANES, (c + 1) * LANES)
            xf[c] = recv_a[slabs, :, cols].astype(F32).reshape(SLABS * WIN, LANES)

        def four(j, carry):
            def load():
                return jnp.concatenate(
                    [
                        jnp.concatenate(
                            [xf[c, pl.ds(j * GROUP + w, SPAN, stride=WIN), :] for c in range(D // LANES)],
                            axis=1,
                        )
                        for w in range(GROUP)
                    ],
                    axis=0,
                )

            result = attend(load, g2, wq2, wo2, q_s, k_s, v_s, mixed_s)
            for w in range(GROUP):
                for c in range(D // LANES):
                    yf[c, pl.ds(j * GROUP + w, SPAN, stride=WIN), :] = result[
                        w * SPAN : (w + 1) * SPAN, c * LANES : (c + 1) * LANES
                    ]
            return carry

        lax.fori_loop(0, 2, four, 0)
        dst = out.at[pl.ds((half * WIN + lon) * LONS + parity * ZHALF + z // 2, 1)]

        def forward(j, carry):
            part = pl.ds(pl.multiple_of(j * ROWS, ROWS), ROWS)

            def load():
                return jnp.concatenate([yf[c, part, :] for c in range(D // LANES)], axis=1).astype(BF16).astype(F32)

            normed = norm(load(), g3[...])
            total = load()
            for f in range(FF // D):
                cols = slice(f * D, (f + 1) * D)
                hidden = jax.nn.gelu(
                    jnp.dot(normed, wu[:, cols], preferred_element_type=F32), approximate=True
                ).astype(BF16)
                total = total + jnp.dot(hidden, wd[cols, :], preferred_element_type=F32)
            send_b[pl.ds(half * SLABS + j * (ROWS // WIN), ROWS // WIN)] = (
                total.astype(BF16).reshape(ROWS // WIN, WIN, D)
            )

            def sends(i, carry):
                b = j * (LONS // 2) + i
                plon = lax.rem(lon - b + LONS, LONS)
                for off in Z_OFFSETS:
                    pz = around(off)
                    src = send_b.at[pl.ds(half * SLABS + b * ZN + pz, 1)]
                    if off:
                        push(src, dst, sb, rb, pz, plon)
                    else:
                        push_or_keep(b == 0, src, dst, sb, rb, pz, plon)
                return carry

            lax.fori_loop(0, LONS // 2, sends, 0)
            return carry

        lax.fori_loop(0, 2, forward, 0)
        return carry

    lax.fori_loop(0, HALVES, grid_phase, 0)

    arrived(out, rb)
    gone = send_a.at[pl.ds(0, HALVES * (SLABS - 1))]
    arrived(gone, sa)
    arrived(gone, sb)


def shards(
    tokens, block_gain, block_qkv, block_out, grid_gain, grid_qkv, grid_out, mlp_gain, w_up, w_down
):
    rows, cols, width = tokens.shape
    slabs = HALVES * SLABS
    any_spec = pl.BlockSpec(memory_space=pl.ANY)
    vmem = pltpu.VMEM
    result = pl.pallas_call(
        kernel,
        out_shape=jax.ShapeDtypeStruct((slabs, WIN, D), BF16),
        in_specs=[any_spec] * 10,
        out_specs=any_spec,
        scratch_shapes=[
            vmem((rows, cols, D), BF16),
            vmem((1, D), F32), vmem((D, 3 * D), BF16), vmem((D, D), BF16),
            vmem((1, D), F32), vmem((D, 3 * D), BF16), vmem((D, D), BF16),
            vmem((1, D), F32), vmem((D, FF), BF16), vmem((FF, D), BF16),
            vmem((ROWS, D), BF16), vmem((ROWS, D), BF16), vmem((ROWS, D), BF16), vmem((ROWS, D), BF16),
            vmem((D // LANES, SLABS * WIN, LANES), F32), vmem((D // LANES, SLABS * WIN, LANES), F32),
            vmem((slabs, WIN, D), BF16), vmem((slabs, WIN, D), BF16), vmem((slabs, WIN, D), BF16),
            pltpu.SemaphoreType.DMA((QUARTERS + 9,)),
            pltpu.SemaphoreType.DMA,
            pltpu.SemaphoreType.DMA((HALVES,)),
            pltpu.SemaphoreType.DMA,
            pltpu.SemaphoreType.DMA,
        ],
        compiler_params=pltpu.CompilerParams(
            collective_id=0, has_side_effects=True, vmem_limit_bytes=48 << 20
        ),
    )(*[pltpu.with_memory_space_constraint(a, pltpu.HBM) for a in (
        tokens, block_gain.reshape(1, D), block_qkv, block_out, grid_gain.reshape(1, D), grid_qkv, grid_out,
        mlp_gain.reshape(1, D), w_up, w_down,
    )])
    return result.reshape(tokens.shape)


def solution(mesh):
    in_specs = (P(("samp", "lat"), "lon", None), P(), P(), P(), P(), P(), P(), P(), P(), P())
    out_specs = P(("samp", "lat"), "lon", None)
    return jax.shard_map(shards, mesh=mesh, in_specs=in_specs, out_specs=out_specs, check_vma=False)
```

```python
import math

import jax
import jax.numpy as jnp
from jax import lax
from jax.experimental import pallas as pl
from jax.experimental.pallas import tpu as pltpu
from jax.sharding import PartitionSpec as P

MESH = pl.DeviceIdType.MESH
BF16 = jnp.bfloat16
F32 = jnp.float32

HEADS = 16
WIN = 8
D = 512
FF = 2048
HEAD = D // HEADS
SPAN = WIN * WIN
HALVES = 2
GROUP = 4
ROWS = GROUP * SPAN
QUARTERS = 4
ZN = 8
ZHALF = 4
LONS = 8
YN = 4
SLABS = ZN * LONS
Z_OFFSETS = (4, 3, -3, 2, -2, 1, -1, 0)
LANES = 128
QUAD = LANES // HEAD
SCALE = math.log2(math.e) / math.sqrt(HEAD)


def norm(x, gain):
    mean = jnp.mean(x, axis=-1, keepdims=True)
    centred = x - mean
    spread = jnp.mean(centred * centred, axis=-1, keepdims=True)
    return (centred * lax.rsqrt(spread + 1e-05) * gain).astype(BF16)


def head_masks():
    lane = lax.broadcasted_iota(jnp.int32, (SPAN, LANES), 1)
    return [(lane >= h * HEAD) & (lane < (h + 1) * HEAD) for h in range(QUAD)]


def attend(load, gain, w_qkv, w_out, q_s, k_s, v_s, mixed_s):
    normed = norm(load(), gain[...])
    q_s[...] = (jnp.dot(normed, w_qkv[:, :D], preferred_element_type=F32) * SCALE).astype(BF16)
    k_s[...] = jnp.dot(normed, w_qkv[:, D : 2 * D], preferred_element_type=F32).astype(BF16)
    v_s[...] = jnp.dot(normed, w_qkv[:, 2 * D :], preferred_element_type=F32).astype(BF16)
    masks = head_masks()
    for w in range(GROUP):
        rows = slice(w * SPAN, (w + 1) * SPAN)
        for g in range(HEADS // QUAD):
            cols = slice(g * LANES, (g + 1) * LANES)
            q = q_s[rows, cols]
            diagonal = jnp.concatenate([jnp.where(m, q, jnp.zeros_like(q)) for m in masks], axis=0)
            scores = lax.dot_general(
                k_s[rows, cols], diagonal, (((1,), (1,)), ((), ())), preferred_element_type=F32
            )
            probs = jnp.exp2(scores - jnp.max(scores, axis=0, keepdims=True))
            probs = (probs * (1.0 / jnp.sum(probs, axis=0, keepdims=True))).astype(BF16)
            mixed = lax.dot_general(
                probs, v_s[rows, cols], (((0,), (0,)), ((), ())), preferred_element_type=F32
            )
            kept = mixed[(QUAD - 1) * SPAN :]
            for h in range(QUAD - 1):
                kept = jnp.where(masks[h], mixed[h * SPAN : (h + 1) * SPAN], kept)
            mixed_s[rows, cols] = kept.astype(BF16)
    return load() + jnp.dot(mixed_s[...], w_out[...], preferred_element_type=F32)


def kernel(
    tokens, block_gain, block_qkv, block_out, grid_gain, grid_qkv, grid_out, mlp_gain, w_up, w_down,
    out,
    x_s, g1, wq1, wo1, g2, wq2, wo2, g3, wu, wd,
    q_s, k_s, v_s, mixed_s, xf, yf,
    send_a, recv_a, send_b,
    load_sem, sa, ra, sb, rb, ready,
):
    lat = lax.axis_index("lat")
    lon = lax.axis_index("lon")
    z = lat // 2
    core = lax.rem(lat, 2)

    def peer(pz, plon):
        return {"lat": pz * 2 + core, "lon": plon}

    def quarter_load(q):
        part = (pl.ds(q // 2 * WIN, WIN), pl.ds(q % 2 * GROUP * WIN, GROUP * WIN))
        return pltpu.make_async_copy(tokens.at[part], x_s.at[part], load_sem.at[q])

    def around(off):
        return lax.rem(z + off + ZN, ZN)

    def steps_of_y(b):
        h = b % YN
        return h + h // 2 - 2 * (h // 3)

    def ahead(b):
        return lax.rem(lon // YN + b // YN, 2) * YN + lax.rem(lon % YN + steps_of_y(b), YN)

    def behind(b):
        return lax.rem(lon // YN + b // YN, 2) * YN + lax.rem(lon % YN + YN - steps_of_y(b), YN)

    barrier = pltpu.get_barrier_semaphore()

    for off in Z_OFFSETS[:-1]:
        pl.semaphore_signal(barrier, inc=1, device_id=peer(around(off), lon), device_id_type=MESH)
    for b in range(1, LONS):
        pl.semaphore_signal(barrier, inc=1, device_id=peer(z, ahead(b)), device_id_type=MESH)

    weights = [
        pltpu.make_async_copy(src, dst, load_sem.at[QUARTERS + i])
        for i, (src, dst) in enumerate([
            (block_gain, g1), (block_qkv, wq1), (block_out, wo1),
            (grid_gain, g2), (grid_qkv, wq2), (grid_out, wo2),
            (mlp_gain, g3), (w_up, wu), (w_down, wd),
        ])
    ]
    quarter_load(0).start()
    for copy in weights[:3]:
        copy.start()

    def push(src, dst, send_sem, recv_sem, pz, plon):
        pltpu.make_async_remote_copy(
            src_ref=src, dst_ref=dst, send_sem=send_sem, recv_sem=recv_sem,
            device_id=peer(pz, plon), device_id_type=MESH,
        ).start()

    def push_or_keep(local, src, dst, send_sem, recv_sem, pz, plon):
        @pl.when(local)
        def _():
            pltpu.make_async_copy(src, dst, recv_sem).start()

        @pl.when(jnp.logical_not(local))
        def _():
            push(src, dst, send_sem, recv_sem, pz, plon)

    def arrived(ref, sem):
        pltpu.make_async_copy(ref, ref, sem).wait()

    parity = lax.rem(z, 2)

    def block_phase(q, carry):
        half = q // 2
        side = lax.rem(q, 2)

        @pl.when(q == 0)
        def _():
            for copy in weights[:3]:
                copy.wait()

        for i in range(QUARTERS):
            @pl.when(q == i)
            def _():
                quarter_load(i).wait()

        def load():
            tile = x_s[pl.ds(half * WIN, WIN), pl.ds(pl.multiple_of(side * 32, 32), 32), :].astype(F32)
            return jnp.concatenate(
                [tile[:, w * WIN : (w + 1) * WIN, :].reshape(SPAN, D) for w in range(GROUP)], axis=0
            )

        result = attend(load, g1, wq1, wo1, q_s, k_s, v_s, mixed_s)
        for w in range(GROUP):
            part = result[w * SPAN : (w + 1) * SPAN].reshape(WIN, WIN, D)
            for r in range(WIN):
                send_a[(q * LONS + r) * ZHALF + w] = part[r].astype(BF16)

        @pl.when(q == 0)
        def _():
            pl.semaphore_wait(barrier, ZN + LONS - 2)
            for b in range(1, LONS):
                pl.semaphore_signal(
                    ready.at[b], inc=1, device_id=peer(z, behind(b)), device_id_type=MESH
                )

        def sends(b, carry):
            plon = ahead(b)

            @pl.when((q == 0) & (b > 0))
            def _():
                pl.semaphore_wait(ready.at[b], 1)

            for i in (1, 3, 2, 0):
                w = lax.rem(z // 2 + i, ZHALF)
                src = send_a.at[pl.ds((q * LONS + plon) * ZHALF + w, 1)]
                dst = recv_a.at[pl.ds(half * SLABS + b * ZN + z, 1)]
                if i:
                    push(src, dst, sa, ra.at[half], 2 * w + side, plon)
                else:
                    push_or_keep((b == 0) & (side == parity), src, dst, sa, ra.at[half], 2 * w + side, plon)
            return carry

        @pl.when(q == 0)
        def _():
            for i in range(1, QUARTERS):
                quarter_load(i).start()
            for copy in weights[3:]:
                copy.start()

        lax.fori_loop(0, LONS, sends, 0)
        return carry

    lax.fori_loop(0, QUARTERS, block_phase, 0)

    for copy in weights[3:]:
        copy.wait()

    def grid_phase(half, carry):
        slabs = pl.ds(half * SLABS, SLABS)
        arrived(recv_a.at[slabs], ra.at[half])
        for c in range(D // LANES):
            cols = slice(c * LANES, (c + 1) * LANES)
            xf[c] = recv_a[slabs, :, cols].astype(F32).reshape(SLABS * WIN, LANES)

        def four(j, carry):
            def load():
                return jnp.concatenate(
                    [
                        jnp.concatenate(
                            [xf[c, pl.ds(j * GROUP + w, SPAN, stride=WIN), :] for c in range(D // LANES)],
                            axis=1,
                        )
                        for w in range(GROUP)
                    ],
                    axis=0,
                )

            result = attend(load, g2, wq2, wo2, q_s, k_s, v_s, mixed_s)
            for w in range(GROUP):
                for c in range(D // LANES):
                    yf[c, pl.ds(j * GROUP + w, SPAN, stride=WIN), :] = result[
                        w * SPAN : (w + 1) * SPAN, c * LANES : (c + 1) * LANES
                    ]
            return carry

        lax.fori_loop(0, 2, four, 0)
        dst = out.at[pl.ds((half * WIN + lon) * LONS + parity * ZHALF + z // 2, 1)]

        def forward(step, carry):
            j = 1 - step
            part = pl.ds(pl.multiple_of(j * ROWS, ROWS), ROWS)

            def load():
                return jnp.concatenate([yf[c, part, :] for c in range(D // LANES)], axis=1).astype(BF16).astype(F32)

            normed = norm(load(), g3[...])
            total = load()
            for f in range(FF // D):
                cols = slice(f * D, (f + 1) * D)
                hidden = jax.nn.gelu(
                    jnp.dot(normed, wu[:, cols], preferred_element_type=F32), approximate=True
                ).astype(BF16)
                total = total + jnp.dot(hidden, wd[cols, :], preferred_element_type=F32)
            send_b[pl.ds(half * SLABS + j * (ROWS // WIN), ROWS // WIN)] = (
                total.astype(BF16).reshape(ROWS // WIN, WIN, D)
            )

            def sends(i, carry):
                b = j * (LONS // 2) + LONS // 2 - 1 - i
                plon = behind(b)
                for off in Z_OFFSETS:
                    pz = around(off)
                    src = send_b.at[pl.ds(half * SLABS + b * ZN + pz, 1)]
                    if off:
                        push(src, dst, sb, rb, pz, plon)
                    else:
                        push_or_keep(b == 0, src, dst, sb, rb, pz, plon)
                return carry

            lax.fori_loop(0, LONS // 2, sends, 0)
            return carry

        lax.fori_loop(0, 2, forward, 0)
        return carry

    lax.fori_loop(0, HALVES, grid_phase, 0)

    arrived(out, rb)
    gone = send_a.at[pl.ds(0, HALVES * (SLABS - 1))]
    arrived(gone, sa)
    arrived(gone, sb)


def shards(
    tokens, block_gain, block_qkv, block_out, grid_gain, grid_qkv, grid_out, mlp_gain, w_up, w_down
):
    rows, cols, width = tokens.shape
    slabs = HALVES * SLABS
    any_spec = pl.BlockSpec(memory_space=pl.ANY)
    vmem = pltpu.VMEM
    result = pl.pallas_call(
        kernel,
        out_shape=jax.ShapeDtypeStruct((slabs, WIN, D), BF16),
        in_specs=[any_spec] * 10,
        out_specs=any_spec,
        scratch_shapes=[
            vmem((rows, cols, D), BF16),
            vmem((1, D), F32), vmem((D, 3 * D), BF16), vmem((D, D), BF16),
            vmem((1, D), F32), vmem((D, 3 * D), BF16), vmem((D, D), BF16),
            vmem((1, D), F32), vmem((D, FF), BF16), vmem((FF, D), BF16),
            vmem((ROWS, D), BF16), vmem((ROWS, D), BF16), vmem((ROWS, D), BF16), vmem((ROWS, D), BF16),
            vmem((D // LANES, SLABS * WIN, LANES), F32), vmem((D // LANES, SLABS * WIN, LANES), F32),
            vmem((slabs, WIN, D), BF16), vmem((slabs, WIN, D), BF16), vmem((slabs, WIN, D), BF16),
            pltpu.SemaphoreType.DMA((QUARTERS + 9,)),
            pltpu.SemaphoreType.DMA,
            pltpu.SemaphoreType.DMA((HALVES,)),
            pltpu.SemaphoreType.DMA,
            pltpu.SemaphoreType.DMA,
            pltpu.SemaphoreType.REGULAR((LONS,)),
        ],
        compiler_params=pltpu.CompilerParams(
            collective_id=0, has_side_effects=True, vmem_limit_bytes=48 << 20
        ),
    )(*[pltpu.with_memory_space_constraint(a, pltpu.HBM) for a in (
        tokens, block_gain.reshape(1, D), block_qkv, block_out, grid_gain.reshape(1, D), grid_qkv, grid_out,
        mlp_gain.reshape(1, D), w_up, w_down,
    )])
    return result.reshape(tokens.shape)


def solution(mesh):
    in_specs = (P(("samp", "lat"), "lon", None), P(), P(), P(), P(), P(), P(), P(), P(), P())
    out_specs = P(("samp", "lat"), "lon", None)
    return jax.shard_map(shards, mesh=mesh, in_specs=in_specs, out_specs=out_specs, check_vma=False)
```

```python
import math

import jax
import jax.numpy as jnp
from jax import lax
from jax.experimental import pallas as pl
from jax.experimental.pallas import tpu as pltpu
from jax.sharding import PartitionSpec as P

MESH = pl.DeviceIdType.MESH
BF16 = jnp.bfloat16
F32 = jnp.float32

HEADS = 16
WIN = 8
D = 512
FF = 2048
HEAD = D // HEADS
SPAN = WIN * WIN
HALVES = 2
GROUP = 4
ROWS = GROUP * SPAN
QUARTERS = 4
ZN = 8
ZHALF = 4
LONS = 8
YN = 4
SLABS = ZN * LONS
Z_OFFSETS = (4, 3, -3, 2, -2, 1, -1, 0)
LANES = 128
QUAD = LANES // HEAD
SCALE = math.log2(math.e) / math.sqrt(HEAD)


def norm(x, gain):
    mean = jnp.mean(x, axis=-1, keepdims=True)
    centred = x - mean
    spread = jnp.mean(centred * centred, axis=-1, keepdims=True)
    return (centred * lax.rsqrt(spread + 1e-05) * gain).astype(BF16)


def head_masks():
    lane = lax.broadcasted_iota(jnp.int32, (SPAN, LANES), 1)
    return [(lane >= h * HEAD) & (lane < (h + 1) * HEAD) for h in range(QUAD)]


def attend(load, gain, w_qkv, w_out, q_s, k_s, v_s, mixed_s):
    normed = norm(load(), gain[...])
    q_s[...] = (jnp.dot(normed, w_qkv[:, :D], preferred_element_type=F32) * SCALE).astype(BF16)
    k_s[...] = jnp.dot(normed, w_qkv[:, D : 2 * D], preferred_element_type=F32).astype(BF16)
    v_s[...] = jnp.dot(normed, w_qkv[:, 2 * D :], preferred_element_type=F32).astype(BF16)
    masks = head_masks()
    parts = [
        (slice(w * SPAN, (w + 1) * SPAN), slice(g * LANES, (g + 1) * LANES))
        for w in range(GROUP)
        for g in range(HEADS // QUAD)
    ]
    scores = []
    for part in parts:
        q = q_s[part]
        diagonal = jnp.concatenate([jnp.where(m, q, jnp.zeros_like(q)) for m in masks], axis=0)
        scores.append(
            lax.dot_general(
                k_s[part], diagonal, (((1,), (1,)), ((), ())), preferred_element_type=F32
            )
        )
    probs = []
    for score in scores:
        grown = jnp.exp2(score - jnp.max(score, axis=0, keepdims=True))
        probs.append((grown * (1.0 / jnp.sum(grown, axis=0, keepdims=True))).astype(BF16))
    for part, prob in zip(parts, probs):
        mixed = lax.dot_general(
            prob, v_s[part], (((0,), (0,)), ((), ())), preferred_element_type=F32
        )
        kept = mixed[(QUAD - 1) * SPAN :]
        for h in range(QUAD - 1):
            kept = jnp.where(masks[h], mixed[h * SPAN : (h + 1) * SPAN], kept)
        mixed_s[part] = kept.astype(BF16)
    return load() + jnp.dot(mixed_s[...], w_out[...], preferred_element_type=F32)


def kernel(
    tokens, block_gain, block_qkv, block_out, grid_gain, grid_qkv, grid_out, mlp_gain, w_up, w_down,
    out,
    x_s, g1, wq1, wo1, g2, wq2, wo2, g3, wu, wd,
    q_s, k_s, v_s, mixed_s, xf, yf,
    send_a, recv_a, send_b,
    load_sem, sa, ra, sb, rb, ready,
):
    lat = lax.axis_index("lat")
    lon = lax.axis_index("lon")
    z = lat // 2
    core = lax.rem(lat, 2)

    def peer(pz, plon):
        return {"lat": pz * 2 + core, "lon": plon}

    def quarter_load(q):
        part = (pl.ds(q // 2 * WIN, WIN), pl.ds(q % 2 * GROUP * WIN, GROUP * WIN))
        return pltpu.make_async_copy(tokens.at[part], x_s.at[part], load_sem.at[q])

    def around(off):
        return lax.rem(z + off + ZN, ZN)

    def steps_of_y(b):
        h = b % YN
        return h + h // 2 - 2 * (h // 3)

    def ahead(b):
        return lax.rem(lon // YN + b // YN, 2) * YN + lax.rem(lon % YN + steps_of_y(b), YN)

    def behind(b):
        return lax.rem(lon // YN + b // YN, 2) * YN + lax.rem(lon % YN + YN - steps_of_y(b), YN)

    barrier = pltpu.get_barrier_semaphore()

    for off in Z_OFFSETS[:-1]:
        pl.semaphore_signal(barrier, inc=1, device_id=peer(around(off), lon), device_id_type=MESH)
    for b in range(1, LONS):
        pl.semaphore_signal(barrier, inc=1, device_id=peer(z, ahead(b)), device_id_type=MESH)

    weights = [
        pltpu.make_async_copy(src, dst, load_sem.at[QUARTERS + i])
        for i, (src, dst) in enumerate([
            (block_gain, g1), (block_qkv, wq1), (block_out, wo1),
            (grid_gain, g2), (grid_qkv, wq2), (grid_out, wo2),
            (mlp_gain, g3), (w_up, wu), (w_down, wd),
        ])
    ]
    quarter_load(0).start()
    for copy in weights[:3]:
        copy.start()

    def push(src, dst, send_sem, recv_sem, pz, plon):
        pltpu.make_async_remote_copy(
            src_ref=src, dst_ref=dst, send_sem=send_sem, recv_sem=recv_sem,
            device_id=peer(pz, plon), device_id_type=MESH,
        ).start()

    def push_or_keep(local, src, dst, send_sem, recv_sem, pz, plon):
        @pl.when(local)
        def _():
            pltpu.make_async_copy(src, dst, recv_sem).start()

        @pl.when(jnp.logical_not(local))
        def _():
            push(src, dst, send_sem, recv_sem, pz, plon)

    def arrived(ref, sem):
        pltpu.make_async_copy(ref, ref, sem).wait()

    parity = lax.rem(z, 2)

    def block_phase(q, carry):
        half = q // 2
        side = lax.rem(q, 2)

        @pl.when(q == 0)
        def _():
            for copy in weights[:3]:
                copy.wait()

        for i in range(QUARTERS):
            @pl.when(q == i)
            def _():
                quarter_load(i).wait()

        def load():
            tile = x_s[pl.ds(half * WIN, WIN), pl.ds(pl.multiple_of(side * 32, 32), 32), :].astype(F32)
            return jnp.concatenate(
                [tile[:, w * WIN : (w + 1) * WIN, :].reshape(SPAN, D) for w in range(GROUP)], axis=0
            )

        result = attend(load, g1, wq1, wo1, q_s, k_s, v_s, mixed_s)
        for w in range(GROUP):
            part = result[w * SPAN : (w + 1) * SPAN].reshape(WIN, WIN, D)
            for r in range(WIN):
                send_a[(q * LONS + r) * ZHALF + w] = part[r].astype(BF16)

        @pl.when(q == 0)
        def _():
            pl.semaphore_wait(barrier, ZN + LONS - 2)
            for b in range(1, LONS):
                pl.semaphore_signal(
                    ready.at[b], inc=1, device_id=peer(z, behind(b)), device_id_type=MESH
                )

        def sends(b, carry):
            plon = ahead(b)

            if b:
                @pl.when(q == 0)
                def _():
                    pl.semaphore_wait(ready.at[b], 1)

            for i in (1, 3, 2, 0):
                w = lax.rem(z // 2 + i, ZHALF)
                src = send_a.at[pl.ds((q * LONS + plon) * ZHALF + w, 1)]
                dst = recv_a.at[pl.ds(half * SLABS + b * ZN + z, 1)]
                if i or b:
                    push(src, dst, sa, ra.at[half], 2 * w + side, plon)
                else:
                    push_or_keep(side == parity, src, dst, sa, ra.at[half], 2 * w + side, plon)
            return carry

        @pl.when(q == 0)
        def _():
            for i in range(1, QUARTERS):
                quarter_load(i).start()
            for copy in weights[3:]:
                copy.start()

        for b in range(LONS):
            sends(b, 0)
        return carry

    lax.fori_loop(0, QUARTERS, block_phase, 0)

    for copy in weights[3:]:
        copy.wait()

    def grid_phase(half, carry):
        slabs = pl.ds(half * SLABS, SLABS)
        arrived(recv_a.at[slabs], ra.at[half])
        for c in range(D // LANES):
            cols = slice(c * LANES, (c + 1) * LANES)
            xf[c] = recv_a[slabs, :, cols].astype(F32).reshape(SLABS * WIN, LANES)

        def four(j, carry):
            def load():
                return jnp.concatenate(
                    [
                        jnp.concatenate(
                            [xf[c, pl.ds(j * GROUP + w, SPAN, stride=WIN), :] for c in range(D // LANES)],
                            axis=1,
                        )
                        for w in range(GROUP)
                    ],
                    axis=0,
                )

            result = attend(load, g2, wq2, wo2, q_s, k_s, v_s, mixed_s)
            for w in range(GROUP):
                for c in range(D // LANES):
                    yf[c, pl.ds(j * GROUP + w, SPAN, stride=WIN), :] = result[
                        w * SPAN : (w + 1) * SPAN, c * LANES : (c + 1) * LANES
                    ]
            return carry

        lax.fori_loop(0, 2, four, 0)
        dst = out.at[pl.ds((half * WIN + lon) * LONS + parity * ZHALF + z // 2, 1)]

        def forward(step, carry):
            j = 1 - step
            part = pl.ds(pl.multiple_of(j * ROWS, ROWS), ROWS)

            def load():
                return jnp.concatenate([yf[c, part, :] for c in range(D // LANES)], axis=1).astype(BF16).astype(F32)

            normed = norm(load(), g3[...])
            total = load()
            for f in range(FF // D):
                cols = slice(f * D, (f + 1) * D)
                hidden = jax.nn.gelu(
                    jnp.dot(normed, wu[:, cols], preferred_element_type=F32), approximate=True
                ).astype(BF16)
                total = total + jnp.dot(hidden, wd[cols, :], preferred_element_type=F32)
            send_b[pl.ds(half * SLABS + j * (ROWS // WIN), ROWS // WIN)] = (
                total.astype(BF16).reshape(ROWS // WIN, WIN, D)
            )

            def sends(i, carry):
                b = j * (LONS // 2) + LONS // 2 - 1 - i
                plon = behind(b)
                for off in Z_OFFSETS:
                    pz = around(off)
                    src = send_b.at[pl.ds(half * SLABS + b * ZN + pz, 1)]
                    if off:
                        push(src, dst, sb, rb, pz, plon)
                    else:
                        push_or_keep(b == 0, src, dst, sb, rb, pz, plon)
                return carry

            lax.fori_loop(0, LONS // 2, sends, 0)
            return carry

        lax.fori_loop(0, 2, forward, 0)
        return carry

    lax.fori_loop(0, HALVES, grid_phase, 0)

    arrived(out, rb)
    gone = send_a.at[pl.ds(0, HALVES * (SLABS - 1))]
    arrived(gone, sa)
    arrived(gone, sb)


def shards(
    tokens, block_gain, block_qkv, block_out, grid_gain, grid_qkv, grid_out, mlp_gain, w_up, w_down
):
    rows, cols, width = tokens.shape
    slabs = HALVES * SLABS
    any_spec = pl.BlockSpec(memory_space=pl.ANY)
    vmem = pltpu.VMEM
    result = pl.pallas_call(
        kernel,
        out_shape=jax.ShapeDtypeStruct((slabs, WIN, D), BF16),
        in_specs=[any_spec] * 10,
        out_specs=any_spec,
        scratch_shapes=[
            vmem((rows, cols, D), BF16),
            vmem((1, D), F32), vmem((D, 3 * D), BF16), vmem((D, D), BF16),
            vmem((1, D), F32), vmem((D, 3 * D), BF16), vmem((D, D), BF16),
            vmem((1, D), F32), vmem((D, FF), BF16), vmem((FF, D), BF16),
            vmem((ROWS, D), BF16), vmem((ROWS, D), BF16), vmem((ROWS, D), BF16), vmem((ROWS, D), BF16),
            vmem((D // LANES, SLABS * WIN, LANES), F32), vmem((D // LANES, SLABS * WIN, LANES), F32),
            vmem((slabs, WIN, D), BF16), vmem((slabs, WIN, D), BF16), vmem((slabs, WIN, D), BF16),
            pltpu.SemaphoreType.DMA((QUARTERS + 9,)),
            pltpu.SemaphoreType.DMA,
            pltpu.SemaphoreType.DMA((HALVES,)),
            pltpu.SemaphoreType.DMA,
            pltpu.SemaphoreType.DMA,
            pltpu.SemaphoreType.REGULAR((LONS,)),
        ],
        compiler_params=pltpu.CompilerParams(
            collective_id=0, has_side_effects=True, vmem_limit_bytes=48 << 20
        ),
    )(*[pltpu.with_memory_space_constraint(a, pltpu.HBM) for a in (
        tokens, block_gain.reshape(1, D), block_qkv, block_out, grid_gain.reshape(1, D), grid_qkv, grid_out,
        mlp_gain.reshape(1, D), w_up, w_down,
    )])
    return result.reshape(tokens.shape)


def solution(mesh):
    in_specs = (P(("samp", "lat"), "lon", None), P(), P(), P(), P(), P(), P(), P(), P(), P())
    out_specs = P(("samp", "lat"), "lon", None)
    return jax.shard_map(shards, mesh=mesh, in_specs=in_specs, out_specs=out_specs, check_vma=False)
```

```python
import math

import jax
import jax.numpy as jnp
from jax import lax
from jax.experimental import pallas as pl
from jax.experimental.pallas import tpu as pltpu
from jax.sharding import PartitionSpec as P

MESH = pl.DeviceIdType.MESH
BF16 = jnp.bfloat16
F32 = jnp.float32

HEADS = 16
WIN = 8
D = 512
FF = 2048
HEAD = D // HEADS
SPAN = WIN * WIN
HALVES = 2
GROUP = 4
ROWS = GROUP * SPAN
QUARTERS = 4
ZN = 8
ZHALF = 4
LONS = 8
YN = 4
SLABS = ZN * LONS
Z_OFFSETS = (4, 3, -3, 2, -2, 1, -1, 0)
LANES = 128
QUAD = LANES // HEAD
SCALE = math.log2(math.e) / math.sqrt(HEAD)


def norm(x, gain):
    mean = jnp.mean(x, axis=-1, keepdims=True)
    centred = x - mean
    spread = jnp.mean(centred * centred, axis=-1, keepdims=True)
    return (centred * lax.rsqrt(spread + 1e-05) * gain).astype(BF16)


def head_masks():
    lane = lax.broadcasted_iota(jnp.int32, (SPAN, LANES), 1)
    return [(lane >= h * HEAD) & (lane < (h + 1) * HEAD) for h in range(QUAD)]


def attend(load, gain, w_qkv, w_out, q_s, k_s, v_s, mixed_s, before_out=lambda: None):
    normed = norm(load(), gain[...])
    q_s[...] = (jnp.dot(normed, w_qkv[:, :D], preferred_element_type=F32) * SCALE).astype(BF16)
    k_s[...] = jnp.dot(normed, w_qkv[:, D : 2 * D], preferred_element_type=F32).astype(BF16)
    v_s[...] = jnp.dot(normed, w_qkv[:, 2 * D :], preferred_element_type=F32).astype(BF16)
    masks = head_masks()
    parts = [
        (slice(w * SPAN, (w + 1) * SPAN), slice(g * LANES, (g + 1) * LANES))
        for w in range(GROUP)
        for g in range(HEADS // QUAD)
    ]
    scores = []
    for part in parts:
        q = q_s[part]
        diagonal = jnp.concatenate([jnp.where(m, q, jnp.zeros_like(q)) for m in masks], axis=0)
        scores.append(
            lax.dot_general(
                k_s[part], diagonal, (((1,), (1,)), ((), ())), preferred_element_type=F32
            )
        )
    probs = []
    for score in scores:
        grown = jnp.exp2(score - jnp.max(score, axis=0, keepdims=True))
        probs.append((grown * (1.0 / jnp.sum(grown, axis=0, keepdims=True))).astype(BF16))
    for part, prob in zip(parts, probs):
        mixed = lax.dot_general(
            prob, v_s[part], (((0,), (0,)), ((), ())), preferred_element_type=F32
        )
        kept = mixed[(QUAD - 1) * SPAN :]
        for h in range(QUAD - 1):
            kept = jnp.where(masks[h], mixed[h * SPAN : (h + 1) * SPAN], kept)
        mixed_s[part] = kept.astype(BF16)
    before_out()
    return load() + jnp.dot(mixed_s[...], w_out[...], preferred_element_type=F32)


def kernel(
    tokens, block_gain, block_qkv, block_out, grid_gain, grid_qkv, grid_out, mlp_gain, w_up, w_down,
    out,
    x_s, g1, wq1, wo1, g2, wq2, wo2, g3, wu, wd,
    q_s, k_s, v_s, mixed_s, xf, yf,
    send_a, recv_a, send_b,
    load_sem, sa, ra, sb, rb, ready,
):
    lat = lax.axis_index("lat")
    lon = lax.axis_index("lon")
    z = lat // 2
    core = lax.rem(lat, 2)

    def peer(pz, plon):
        return {"lat": pz * 2 + core, "lon": plon}

    def quarter_load(q):
        part = (pl.ds(q // 2 * WIN, WIN), pl.ds(q % 2 * GROUP * WIN, GROUP * WIN))
        return pltpu.make_async_copy(tokens.at[part], x_s.at[part], load_sem.at[q])

    def around(off):
        return lax.rem(z + off + ZN, ZN)

    def steps_of_y(b):
        h = b % YN
        return h + h // 2 - 2 * (h // 3)

    def ahead(b):
        return lax.rem(lon // YN + b // YN, 2) * YN + lax.rem(lon % YN + steps_of_y(b), YN)

    def behind(b):
        return lax.rem(lon // YN + b // YN, 2) * YN + lax.rem(lon % YN + YN - steps_of_y(b), YN)

    barrier = pltpu.get_barrier_semaphore()

    for off in Z_OFFSETS[:-1]:
        pl.semaphore_signal(barrier, inc=1, device_id=peer(around(off), lon), device_id_type=MESH)
    for b in range(1, LONS):
        pl.semaphore_signal(barrier, inc=1, device_id=peer(z, ahead(b)), device_id_type=MESH)

    weights = [
        pltpu.make_async_copy(src, dst, load_sem.at[QUARTERS + i])
        for i, (src, dst) in enumerate([
            (block_gain, g1), (block_qkv, wq1), (block_out, wo1),
            (grid_gain, g2), (grid_qkv, wq2), (grid_out, wo2),
            (mlp_gain, g3), (w_up, wu), (w_down, wd),
        ])
    ]
    quarter_load(0).start()
    for copy in weights[:3]:
        copy.start()

    def push(src, dst, send_sem, recv_sem, pz, plon):
        pltpu.make_async_remote_copy(
            src_ref=src, dst_ref=dst, send_sem=send_sem, recv_sem=recv_sem,
            device_id=peer(pz, plon), device_id_type=MESH,
        ).start()

    def push_or_keep(local, src, dst, send_sem, recv_sem, pz, plon):
        @pl.when(local)
        def _():
            pltpu.make_async_copy(src, dst, recv_sem).start()

        @pl.when(jnp.logical_not(local))
        def _():
            push(src, dst, send_sem, recv_sem, pz, plon)

    def arrived(ref, sem):
        pltpu.make_async_copy(ref, ref, sem).wait()

    parity = lax.rem(z, 2)

    def block_phase(q, carry):
        half = q // 2
        side = lax.rem(q, 2)

        @pl.when(q == 0)
        def _():
            for copy in weights[:3]:
                copy.wait()

        for i in range(QUARTERS):
            @pl.when(q == i)
            def _():
                quarter_load(i).wait()

        def load():
            tile = x_s[pl.ds(half * WIN, WIN), pl.ds(pl.multiple_of(side * 32, 32), 32), :].astype(F32)
            return jnp.concatenate(
                [tile[:, w * WIN : (w + 1) * WIN, :].reshape(SPAN, D) for w in range(GROUP)], axis=0
            )

        def entry():
            @pl.when(q == 0)
            def _():
                pl.semaphore_wait(barrier, ZN + LONS - 2)
                for b in range(1, LONS):
                    pl.semaphore_signal(
                        ready.at[b], inc=1, device_id=peer(z, behind(b)), device_id_type=MESH
                    )

        result = attend(load, g1, wq1, wo1, q_s, k_s, v_s, mixed_s, entry)
        for w in range(GROUP):
            part = result[w * SPAN : (w + 1) * SPAN].reshape(WIN, WIN, D)
            for r in range(WIN):
                send_a[(q * LONS + r) * ZHALF + w] = part[r].astype(BF16)

        def sends(b, carry):
            plon = ahead(b)

            if b:
                @pl.when(q == 0)
                def _():
                    pl.semaphore_wait(ready.at[b], 1)

            for i in (1, 3, 2, 0):
                w = lax.rem(z // 2 + i, ZHALF)
                src = send_a.at[pl.ds((q * LONS + plon) * ZHALF + w, 1)]
                dst = recv_a.at[pl.ds(half * SLABS + b * ZN + z, 1)]
                if i or b:
                    push(src, dst, sa, ra.at[half], 2 * w + side, plon)
                else:
                    push_or_keep(side == parity, src, dst, sa, ra.at[half], 2 * w + side, plon)
            return carry

        @pl.when(q == 0)
        def _():
            for i in range(1, QUARTERS):
                quarter_load(i).start()
            for copy in weights[3:]:
                copy.start()

        for b in range(LONS):
            sends(b, 0)
        return carry

    lax.fori_loop(0, QUARTERS, block_phase, 0)

    for copy in weights[3:]:
        copy.wait()

    def grid_phase(half, carry):
        slabs = pl.ds(half * SLABS, SLABS)
        arrived(recv_a.at[slabs], ra.at[half])
        for c in range(D // LANES):
            cols = slice(c * LANES, (c + 1) * LANES)
            xf[c] = recv_a[slabs, :, cols].astype(F32).reshape(SLABS * WIN, LANES)

        def four(j, carry):
            def load():
                return jnp.concatenate(
                    [
                        jnp.concatenate(
                            [xf[c, pl.ds(j * GROUP + w, SPAN, stride=WIN), :] for c in range(D // LANES)],
                            axis=1,
                        )
                        for w in range(GROUP)
                    ],
                    axis=0,
                )

            result = attend(load, g2, wq2, wo2, q_s, k_s, v_s, mixed_s)
            for w in range(GROUP):
                for c in range(D // LANES):
                    yf[c, pl.ds(j * GROUP + w, SPAN, stride=WIN), :] = result[
                        w * SPAN : (w + 1) * SPAN, c * LANES : (c + 1) * LANES
                    ]
            return carry

        lax.fori_loop(0, 2, four, 0)
        dst = out.at[pl.ds((half * WIN + lon) * LONS + parity * ZHALF + z // 2, 1)]

        def forward(step, carry):
            j = 1 - step
            part = pl.ds(pl.multiple_of(j * ROWS, ROWS), ROWS)

            def load():
                return jnp.concatenate([yf[c, part, :] for c in range(D // LANES)], axis=1).astype(BF16).astype(F32)

            normed = norm(load(), g3[...])
            total = load()
            for f in range(FF // D):
                cols = slice(f * D, (f + 1) * D)
                hidden = jax.nn.gelu(
                    jnp.dot(normed, wu[:, cols], preferred_element_type=F32), approximate=True
                ).astype(BF16)
                total = total + jnp.dot(hidden, wd[cols, :], preferred_element_type=F32)
            send_b[pl.ds(half * SLABS + j * (ROWS // WIN), ROWS // WIN)] = (
                total.astype(BF16).reshape(ROWS // WIN, WIN, D)
            )

            for off in Z_OFFSETS:
                pz = around(off)
                for i in range(LONS // 2):
                    b = j * (LONS // 2) + LONS // 2 - 1 - i
                    src = send_b.at[pl.ds(half * SLABS + b * ZN + pz, 1)]
                    if off:
                        push(src, dst, sb, rb, pz, behind(b))
                    else:
                        push_or_keep(b == 0, src, dst, sb, rb, pz, behind(b))
            return carry

        lax.fori_loop(0, 2, forward, 0)
        return carry

    lax.fori_loop(0, HALVES, grid_phase, 0)

    arrived(out, rb)
    gone = send_a.at[pl.ds(0, HALVES * (SLABS - 1))]
    arrived(gone, sa)
    arrived(gone, sb)


def shards(
    tokens, block_gain, block_qkv, block_out, grid_gain, grid_qkv, grid_out, mlp_gain, w_up, w_down
):
    rows, cols, width = tokens.shape
    slabs = HALVES * SLABS
    any_spec = pl.BlockSpec(memory_space=pl.ANY)
    vmem = pltpu.VMEM
    result = pl.pallas_call(
        kernel,
        out_shape=jax.ShapeDtypeStruct((slabs, WIN, D), BF16),
        in_specs=[any_spec] * 10,
        out_specs=any_spec,
        scratch_shapes=[
            vmem((rows, cols, D), BF16),
            vmem((1, D), F32), vmem((D, 3 * D), BF16), vmem((D, D), BF16),
            vmem((1, D), F32), vmem((D, 3 * D), BF16), vmem((D, D), BF16),
            vmem((1, D), F32), vmem((D, FF), BF16), vmem((FF, D), BF16),
            vmem((ROWS, D), BF16), vmem((ROWS, D), BF16), vmem((ROWS, D), BF16), vmem((ROWS, D), BF16),
            vmem((D // LANES, SLABS * WIN, LANES), F32), vmem((D // LANES, SLABS * WIN, LANES), F32),
            vmem((slabs, WIN, D), BF16), vmem((slabs, WIN, D), BF16), vmem((slabs, WIN, D), BF16),
            pltpu.SemaphoreType.DMA((QUARTERS + 9,)),
            pltpu.SemaphoreType.DMA,
            pltpu.SemaphoreType.DMA((HALVES,)),
            pltpu.SemaphoreType.DMA,
            pltpu.SemaphoreType.DMA,
            pltpu.SemaphoreType.REGULAR((LONS,)),
        ],
        compiler_params=pltpu.CompilerParams(
            collective_id=0, has_side_effects=True, vmem_limit_bytes=48 << 20
        ),
    )(*[pltpu.with_memory_space_constraint(a, pltpu.HBM) for a in (
        tokens, block_gain.reshape(1, D), block_qkv, block_out, grid_gain.reshape(1, D), grid_qkv, grid_out,
        mlp_gain.reshape(1, D), w_up, w_down,
    )])
    return result.reshape(tokens.shape)


def solution(mesh):
    in_specs = (P(("samp", "lat"), "lon", None), P(), P(), P(), P(), P(), P(), P(), P(), P())
    out_specs = P(("samp", "lat"), "lon", None)
    return jax.shard_map(shards, mesh=mesh, in_specs=in_specs, out_specs=out_specs, check_vma=False)
```

```python
import math

import jax
import jax.numpy as jnp
from jax import lax
from jax.experimental import pallas as pl
from jax.experimental.pallas import tpu as pltpu
from jax.sharding import PartitionSpec as P

MESH = pl.DeviceIdType.MESH
BF16 = jnp.bfloat16
F32 = jnp.float32

HEADS = 16
WIN = 8
D = 512
FF = 2048
HEAD = D // HEADS
SPAN = WIN * WIN
HALVES = 2
GROUP = 4
ROWS = GROUP * SPAN
QUARTERS = 4
ZN = 8
ZHALF = 4
LONS = 8
YN = 4
SLABS = ZN * LONS
Z_OFFSETS = (4, 3, -3, 2, -2, 1, -1, 0)
LANES = 128
QUAD = LANES // HEAD
SCALE = math.log2(math.e) / math.sqrt(HEAD)


def norm(x, gain):
    mean = jnp.mean(x, axis=-1, keepdims=True)
    centred = x - mean
    spread = jnp.mean(centred * centred, axis=-1, keepdims=True)
    return (centred * lax.rsqrt(spread + 1e-05) * gain).astype(BF16)


def head_masks():
    lane = lax.broadcasted_iota(jnp.int32, (SPAN, LANES), 1)
    return [(lane >= h * HEAD) & (lane < (h + 1) * HEAD) for h in range(QUAD)]


def attend(load, gain, w_qkv, w_out, q_s, k_s, v_s, mixed_s, before_out=lambda: None):
    normed = norm(load(), gain[...])
    q_s[...] = (jnp.dot(normed, w_qkv[:, :D], preferred_element_type=F32) * SCALE).astype(BF16)
    k_s[...] = jnp.dot(normed, w_qkv[:, D : 2 * D], preferred_element_type=F32).astype(BF16)
    v_s[...] = jnp.dot(normed, w_qkv[:, 2 * D :], preferred_element_type=F32).astype(BF16)
    masks = head_masks()
    parts = [
        (slice(w * SPAN, (w + 1) * SPAN), slice(g * LANES, (g + 1) * LANES))
        for w in range(GROUP)
        for g in range(HEADS // QUAD)
    ]
    scores = []
    for part in parts:
        q = q_s[part]
        diagonal = jnp.concatenate([jnp.where(m, q, jnp.zeros_like(q)) for m in masks], axis=0)
        scores.append(
            lax.dot_general(
                k_s[part], diagonal, (((1,), (1,)), ((), ())), preferred_element_type=F32
            )
        )
    probs = []
    for score in scores:
        grown = jnp.exp2(score - jnp.max(score, axis=0, keepdims=True))
        probs.append((grown * (1.0 / jnp.sum(grown, axis=0, keepdims=True))).astype(BF16))
    for part, prob in zip(parts, probs):
        mixed = lax.dot_general(
            prob, v_s[part], (((0,), (0,)), ((), ())), preferred_element_type=F32
        )
        kept = mixed[(QUAD - 1) * SPAN :]
        for h in range(QUAD - 1):
            kept = jnp.where(masks[h], mixed[h * SPAN : (h + 1) * SPAN], kept)
        mixed_s[part] = kept.astype(BF16)
    before_out()
    return load() + jnp.dot(mixed_s[...], w_out[...], preferred_element_type=F32)


def kernel(
    tokens, block_gain, block_qkv, block_out, grid_gain, grid_qkv, grid_out, mlp_gain, w_up, w_down,
    out,
    x_s, g1, wq1, wo1, g2, wq2, wo2, g3, wu, wd,
    q_s, k_s, v_s, mixed_s, xf, yf,
    send_a, recv_a, send_b,
    load_sem, sa, ra, sb, rb, ready,
):
    lat = lax.axis_index("lat")
    lon = lax.axis_index("lon")
    z = lat // 2
    core = lax.rem(lat, 2)

    def peer(pz, plon):
        return {"lat": pz * 2 + core, "lon": plon}

    def quarter_load(q):
        part = (pl.ds(q // 2 * WIN, WIN), pl.ds(q % 2 * GROUP * WIN, GROUP * WIN))
        return pltpu.make_async_copy(tokens.at[part], x_s.at[part], load_sem.at[q])

    def around(off):
        return lax.rem(z + off + ZN, ZN)

    def steps_of_y(b):
        h = b % YN
        return h + h // 2 - 2 * (h // 3)

    def ahead(b):
        return lax.rem(lon // YN + b // YN, 2) * YN + lax.rem(lon % YN + steps_of_y(b), YN)

    def behind(b):
        return lax.rem(lon // YN + b // YN, 2) * YN + lax.rem(lon % YN + YN - steps_of_y(b), YN)

    barrier = pltpu.get_barrier_semaphore()

    for off in Z_OFFSETS[:-1]:
        pl.semaphore_signal(barrier, inc=1, device_id=peer(around(off), lon), device_id_type=MESH)
    for b in range(1, LONS):
        pl.semaphore_signal(barrier, inc=1, device_id=peer(z, ahead(b)), device_id_type=MESH)

    weights = [
        pltpu.make_async_copy(src, dst, load_sem.at[QUARTERS + i])
        for i, (src, dst) in enumerate([
            (block_gain, g1), (block_qkv, wq1), (block_out, wo1),
            (grid_gain, g2), (grid_qkv, wq2), (grid_out, wo2),
            (mlp_gain, g3), (w_up, wu), (w_down, wd),
        ])
    ]
    quarter_load(0).start()
    for copy in weights[:3]:
        copy.start()

    def push(src, dst, send_sem, recv_sem, pz, plon):
        pltpu.make_async_remote_copy(
            src_ref=src, dst_ref=dst, send_sem=send_sem, recv_sem=recv_sem,
            device_id=peer(pz, plon), device_id_type=MESH,
        ).start()

    def push_or_keep(local, src, dst, send_sem, recv_sem, pz, plon):
        @pl.when(local)
        def _():
            pltpu.make_async_copy(src, dst, recv_sem).start()

        @pl.when(jnp.logical_not(local))
        def _():
            push(src, dst, send_sem, recv_sem, pz, plon)

    def arrived(ref, sem):
        pltpu.make_async_copy(ref, ref, sem).wait()

    parity = lax.rem(z, 2)

    def block_phase(q, carry):
        half = q // 2
        side = lax.rem(q, 2)

        @pl.when(q == 0)
        def _():
            for copy in weights[:3]:
                copy.wait()

        for i in range(QUARTERS):
            @pl.when(q == i)
            def _():
                quarter_load(i).wait()

        def load():
            tile = x_s[pl.ds(half * WIN, WIN), pl.ds(pl.multiple_of(side * 32, 32), 32), :].astype(F32)
            return jnp.concatenate(
                [tile[:, w * WIN : (w + 1) * WIN, :].reshape(SPAN, D) for w in range(GROUP)], axis=0
            )

        def entry():
            @pl.when(q == 0)
            def _():
                pl.semaphore_wait(barrier, ZN + LONS - 2)
                for b in range(1, LONS):
                    pl.semaphore_signal(
                        ready.at[b], inc=1, device_id=peer(z, behind(b)), device_id_type=MESH
                    )

        result = attend(load, g1, wq1, wo1, q_s, k_s, v_s, mixed_s, entry)
        for w in range(GROUP):
            part = result[w * SPAN : (w + 1) * SPAN].reshape(WIN, WIN, D)
            for r in range(WIN):
                send_a[(q * LONS + r) * ZHALF + w] = part[r].astype(BF16)

        def sends(b, carry):
            plon = ahead(b)

            if b:
                @pl.when(q == 0)
                def _():
                    pl.semaphore_wait(ready.at[b], 1)

            for i in (1, 3, 2, 0):
                w = lax.rem(z // 2 + i, ZHALF)
                src = send_a.at[pl.ds((q * LONS + plon) * ZHALF + w, 1)]
                dst = recv_a.at[pl.ds(half * SLABS + b * ZN + z, 1)]
                if i or b:
                    push(src, dst, sa, ra.at[half], 2 * w + side, plon)
                else:
                    push_or_keep(side == parity, src, dst, sa, ra.at[half], 2 * w + side, plon)
            return carry

        @pl.when(q == 0)
        def _():
            for i in range(1, QUARTERS):
                quarter_load(i).start()
            for copy in weights[3:]:
                copy.start()

        for b in range(LONS):
            sends(b, 0)
        return carry

    lax.fori_loop(0, QUARTERS, block_phase, 0)

    for copy in weights[3:]:
        copy.wait()

    def grid_phase(half, carry):
        slabs = pl.ds(half * SLABS, SLABS)
        arrived(recv_a.at[slabs], ra.at[half])
        for c in range(D // LANES):
            cols = slice(c * LANES, (c + 1) * LANES)
            xf[c] = recv_a[slabs, :, cols].astype(F32).reshape(SLABS * WIN, LANES)

        def four(j, carry):
            def load():
                return jnp.concatenate(
                    [
                        jnp.concatenate(
                            [xf[c, pl.ds(j * GROUP + w, SPAN, stride=WIN), :] for c in range(D // LANES)],
                            axis=1,
                        )
                        for w in range(GROUP)
                    ],
                    axis=0,
                )

            result = attend(load, g2, wq2, wo2, q_s, k_s, v_s, mixed_s)
            for w in range(GROUP):
                for c in range(D // LANES):
                    yf[c, pl.ds(j * GROUP + w, SPAN, stride=WIN), :] = result[
                        w * SPAN : (w + 1) * SPAN, c * LANES : (c + 1) * LANES
                    ]
            return carry

        lax.fori_loop(0, 2, four, 0)
        dst = out.at[pl.ds((half * WIN + lon) * LONS + parity * ZHALF + z // 2, 1)]

        def forward(step, carry):
            j = 1 - step
            part = pl.ds(pl.multiple_of(j * ROWS, ROWS), ROWS)

            def load():
                return jnp.concatenate([yf[c, part, :] for c in range(D // LANES)], axis=1).astype(BF16).astype(F32)

            normed = norm(load(), g3[...])
            total = load()
            for f in range(FF // D):
                cols = slice(f * D, (f + 1) * D)
                hidden = jax.nn.gelu(
                    jnp.dot(normed, wu[:, cols], preferred_element_type=F32), approximate=True
                ).astype(BF16)
                total = total + jnp.dot(hidden, wd[cols, :], preferred_element_type=F32)
            send_b[pl.ds(half * SLABS + j * (ROWS // WIN), ROWS // WIN)] = (
                total.astype(BF16).reshape(ROWS // WIN, WIN, D)
            )

            def sends(i, carry):
                b = j * (LONS // 2) + LONS // 2 - 1 - i
                plon = behind(b)
                for off in Z_OFFSETS:
                    pz = around(off)
                    src = send_b.at[pl.ds(half * SLABS + b * ZN + pz, 1)]
                    if off:
                        push(src, dst, sb, rb, pz, plon)
                    else:
                        push_or_keep(b == 0, src, dst, sb, rb, pz, plon)
                return carry

            lax.fori_loop(0, LONS // 2, sends, 0)
            return carry

        lax.fori_loop(0, 2, forward, 0)
        return carry

    lax.fori_loop(0, HALVES, grid_phase, 0)

    arrived(out, rb)
    gone = send_a.at[pl.ds(0, HALVES * (SLABS - 1))]
    arrived(gone, sa)
    arrived(gone, sb)


def shards(
    tokens, block_gain, block_qkv, block_out, grid_gain, grid_qkv, grid_out, mlp_gain, w_up, w_down
):
    rows, cols, width = tokens.shape
    slabs = HALVES * SLABS
    any_spec = pl.BlockSpec(memory_space=pl.ANY)
    vmem = pltpu.VMEM
    result = pl.pallas_call(
        kernel,
        out_shape=jax.ShapeDtypeStruct((slabs, WIN, D), BF16),
        in_specs=[any_spec] * 10,
        out_specs=any_spec,
        scratch_shapes=[
            vmem((rows, cols, D), BF16),
            vmem((1, D), F32), vmem((D, 3 * D), BF16), vmem((D, D), BF16),
            vmem((1, D), F32), vmem((D, 3 * D), BF16), vmem((D, D), BF16),
            vmem((1, D), F32), vmem((D, FF), BF16), vmem((FF, D), BF16),
            vmem((ROWS, D), BF16), vmem((ROWS, D), BF16), vmem((ROWS, D), BF16), vmem((ROWS, D), BF16),
            vmem((D // LANES, SLABS * WIN, LANES), F32), vmem((D // LANES, SLABS * WIN, LANES), F32),
            vmem((slabs, WIN, D), BF16), vmem((slabs, WIN, D), BF16), vmem((slabs, WIN, D), BF16),
            pltpu.SemaphoreType.DMA((QUARTERS + 9,)),
            pltpu.SemaphoreType.DMA,
            pltpu.SemaphoreType.DMA((HALVES,)),
            pltpu.SemaphoreType.DMA,
            pltpu.SemaphoreType.DMA,
            pltpu.SemaphoreType.REGULAR((LONS,)),
        ],
        compiler_params=pltpu.CompilerParams(
            collective_id=0, has_side_effects=True, vmem_limit_bytes=48 << 20
        ),
    )(*[pltpu.with_memory_space_constraint(a, pltpu.HBM) for a in (
        tokens, block_gain.reshape(1, D), block_qkv, block_out, grid_gain.reshape(1, D), grid_qkv, grid_out,
        mlp_gain.reshape(1, D), w_up, w_down,
    )])
    return result.reshape(tokens.shape)


def solution(mesh):
    in_specs = (P(("samp", "lat"), "lon", None), P(), P(), P(), P(), P(), P(), P(), P(), P())
    out_specs = P(("samp", "lat"), "lon", None)
    return jax.shard_map(shards, mesh=mesh, in_specs=in_specs, out_specs=out_specs, check_vma=False)
```
